256 devices in a mesh: section: 16 (over x, y_hi, core), ulysses: 8 (over z), batch: 2 (over y_lo).
Axes of the slice: x: 4, y: 4 (y_hi: 2, y_lo: 2; y = y_hi * 2 + y_lo), z: 8, core: 2. Of those that a mesh axis runs over, the one named last changes fastest.
Arguments:
- incoming: float32 [32, 512, 3072], P(('batch', 'section'), 'ulysses'), parts along dimension 0, may hold values from -6 to 6
- plan: int32 [16], P('section'), may hold values from 0 to 7
- stale_kv: bfloat16 [32, 4096, 24, 256], P(('batch', 'section'), None, 'ulysses'), parts along dimension 0, may hold values from -60 to 60
- qkv_weight: bfloat16 [16, 3072, 24, 384], P('section', None, 'ulysses'), may hold values from -0.109375 to 0.109375
- out_weight: bfloat16 [16, 24, 128, 3072], P('section', 'ulysses'), may hold values from -0.109375 to 0.109375
- q_gain: float32 [16, 128], P('section'), may hold values from 0.7 to 6
- k_gain: float32 [16, 128], P('section'), may hold values from 0.5 to 1.5
- shift_mod: float32 [16, 3072], P('section'), may hold values from -4 to 4
- scale_mod: float32 [16, 3072], P('section'), may hold values from -2.5 to 2.5
- gate_mod: float32 [16, 3072], P('section'), may hold values from -4 to 4
Outputs:
- block_out: float32 [32, 512, 3072], P(('batch', 'section'), 'ulysses'), parts along dimension 0
- fresh_kv: bfloat16 [32, 512, 24, 256], P(('batch', 'section'), None, 'ulysses'), parts along dimension 0
The draws below stay inside these ranges and needn't reach their ends.
There are 2 independent parts, one for each index of `batch`. The reference program is written for one: setup_inputs(seed, part) draws one part's arguments, and reference() takes and returns one part's arrays. A program takes and returns all parts, laid end to end along the dimension named above; an argument that names none is the same for every part. Nothing has to cross between parts.
All inputs are finite; a program needn't handle non-finite values.
Results may differ from the reference program's by a relative error of at most 0.015.
The reference program's roundings to bfloat16 on the way (of `modulated`, `keys`, `weights` and `attn`) count: a program that leaves them out, or rounds other values in their place, can miss the bound.
Values may be sent and summed in bfloat16 or wider, within the bound.
No kernel may reach another device: no remote copies, remote signals or barrier semaphores. Data moves between devices by JAX's collectives and lax.ppermute only.
A program may use at most 192 MiB of HBM per device.

```python
import math
import jax
import jax.numpy as jnp
from jax import lax

D = 3072
H = 24
DH = 128
P_SIZE = 512
NPATCH = 8
SEQ = 4096
BLOCKS = 16
N_SECTION = 16
N_ULYSSES = 8


def draw_stale_kv(key, part):
    key = jax.random.fold_in(key, 11)
    first = jax.random.fold_in(key, 0)
    shape = (N_SECTION, SEQ, H, 2 * DH)
    values = jnp.clip(jax.random.normal(first, shape, jnp.float32), -6.0, 6.0)
    return values.astype(jnp.bfloat16)


def draw_q_gain(key, part):
    key = jax.random.fold_in(key, 12)
    lower, upper = (0.7, 1.4)
    return jnp.exp(jax.random.uniform(key, (N_SECTION, DH), jnp.float32, math.log(lower), math.log(upper)))


def with_ends(entries, key, low, high):
    index_at = [jax.random.randint(jax.random.fold_in(key, axis), (), 0, length) for axis, length in enumerate(entries.shape)]
    widest = entries.shape.index(max(entries.shape))
    neighbour = index_at[:widest] + [(index_at[widest] + 1) % entries.shape[widest]] + index_at[widest + 1:]
    return entries.at[tuple(index_at)].set(low).at[tuple(neighbour)].set(high)


def shard_levels(key, shape, cuts, least, largest):
    level = 1.0
    for dim, blocks in cuts:
        steps = jax.random.uniform(jax.random.fold_in(jax.random.fold_in(key, 6), dim), (blocks,), jnp.float32, least / len(cuts), largest / len(cuts))
        level = level * jnp.repeat(jnp.exp(steps), shape[dim] // blocks).reshape((-1,) + (1,) * (len(shape) - 1 - dim))
    return level


def normal_values(stream_key, extent, scale, reach, cuts=(), dtype=jnp.bfloat16):
    result = jax.random.normal(stream_key, extent, jnp.float32) * scale
    if len(cuts) > 0:
        result = shard_levels(stream_key, extent, cuts, -0.22, 0.18) * result
    return jnp.clip(result, min=-reach, max=reach).astype(dtype)


def setup_inputs(seed: int = 0, part: int = 0) -> dict:
    streams_of = jax.random.split(jax.random.key(seed), 11)
    part_keys = jax.random.split(jax.random.fold_in(streams_of[10], part), 11)
    return {
        "incoming": normal_values(part_keys[0], (BLOCKS, P_SIZE, D), 1.0, 6.0, ((0, 16), (1, 8)), jnp.float32),
        "plan": with_ends(jax.random.randint(streams_of[1], (BLOCKS,), 0, NPATCH), jax.random.fold_in(streams_of[1], 1), 0, NPATCH - 1).astype(jnp.int32),
        "stale_kv": draw_stale_kv(jax.random.fold_in(jax.random.fold_in(streams_of[10], part), 71), part),
        "qkv_weight": normal_values(streams_of[3], (BLOCKS, D, H, 3 * DH), D ** -0.5, 0.109375, ((0, 16), (2, 8))),
        "out_weight": normal_values(streams_of[4], (BLOCKS, H, DH, D), (H * DH) ** -0.5, 0.109375, ((0, 16), (1, 8))),
        "q_gain": draw_q_gain(jax.random.fold_in(streams_of[10], 71), part),
        "k_gain": jnp.clip(1.0 + 0.1 * jax.random.normal(streams_of[6], (BLOCKS, DH), jnp.float32), 0.5, 1.5),
        "shift_mod": normal_values(streams_of[7], (BLOCKS, D), 1.0, 4.0, ((0, 16),), jnp.float32),
        "scale_mod": normal_values(streams_of[8], (BLOCKS, D), 0.5, 2.5, ((0, 16),), jnp.float32),
        "gate_mod": normal_values(streams_of[9], (BLOCKS, D), 1.0, 4.0, ((0, 16),), jnp.float32),
    }


def normalize(rows, shift_row, scale_row):
    mean = lax.optimization_barrier(jnp.mean(rows, -1, keepdims=True))
    centered = rows - mean
    var = lax.optimization_barrier(jnp.mean(centered * centered, -1, keepdims=True))
    return (centered * lax.rsqrt(var + 1e-06) * (1.0 + scale_row) + shift_row).astype(jnp.bfloat16)

def head_norm(values, gain):
    return values * lax.rsqrt(lax.optimization_barrier(jnp.mean(values * values, -1, keepdims=True)) + 1e-06) * gain

def one_block(operands):
    x, index, buffer, w_qkv, w_out, qg, kg, shift_row, scale_row, gate_row = operands
    modulated = normalize(x, shift_row, scale_row)
    qkv = jnp.dot(modulated, w_qkv.reshape(D, H * 3 * DH), preferred_element_type=jnp.float32).reshape(P_SIZE, H, 3 * DH)
    query = head_norm(qkv[:, :, :DH], qg).astype(jnp.bfloat16)
    keyed = head_norm(qkv[:, :, DH:2 * DH], kg).astype(jnp.bfloat16)
    valued = qkv[:, :, 2 * DH:].astype(jnp.bfloat16)
    fresh = jnp.concatenate([keyed, valued], -1)
    start = (index * P_SIZE).astype(jnp.int32)
    zero = jnp.zeros((), jnp.int32)
    keys = lax.dynamic_update_slice(buffer, fresh, (start, zero, zero))
    scores = jnp.einsum('qhd,khd->hqk', query.astype(jnp.float32), keys[:, :, :DH].astype(jnp.float32)) / math.sqrt(DH)
    weights = jax.nn.softmax(scores, -1).astype(jnp.bfloat16)
    attn = jnp.einsum('hqk,khd->qhd', weights.astype(jnp.float32), keys[:, :, DH:].astype(jnp.float32)).astype(jnp.bfloat16)
    groups = attn.reshape(P_SIZE, N_ULYSSES, H // N_ULYSSES * DH)
    w_groups = w_out.reshape(N_ULYSSES, H // N_ULYSSES * DH, D)
    terms = jnp.einsum('pgc,gcd->gpd', groups.astype(jnp.float32), w_groups.astype(jnp.float32)).astype(jnp.bfloat16)
    terms = lax.optimization_barrier(terms)
    proj = lax.optimization_barrier(jnp.sum(terms.astype(jnp.float32), 0))
    return (x + gate_row * proj, fresh)

def reference(incoming, plan, stale_kv, qkv_weight, out_weight, q_gain, k_gain, shift_mod, scale_mod, gate_mod):
    received = jnp.roll(incoming, 1, axis=0)
    block_out, fresh_kv = lax.map(one_block, (received, plan, stale_kv, qkv_weight, out_weight, q_gain, k_gain, shift_mod, scale_mod, gate_mod))
    return (block_out, fresh_kv)
```

```python
import functools
import math

import jax
import jax.numpy as jnp
from jax import lax
from jax.experimental import pallas as pl
from jax.experimental.pallas import tpu as pltpu
from jax.sharding import PartitionSpec as P

LANES = 128
NT = (((1,), (1,)), ((), ()))
MIB = 2**20


def score_scale(head_size):
    return math.log2(math.e) / math.sqrt(head_size)


def norm_kernel(x_ref, shift_ref, scale_ref, out_ref):
    rows = x_ref[...]
    centered = rows - jnp.mean(rows, -1, keepdims=True)
    var = jnp.mean(centered * centered, -1, keepdims=True)
    out_ref[...] = (
        centered * lax.rsqrt(var + 1e-06) * (1.0 + scale_ref[...]) + shift_ref[...]
    ).astype(jnp.bfloat16)


def normalize(rows, shift_row, scale_row):
    return pl.pallas_call(
        norm_kernel,
        out_shape=jax.ShapeDtypeStruct(rows.shape, jnp.bfloat16),
        cost_estimate=pl.CostEstimate(flops=8 * rows.size, bytes_accessed=6 * rows.size, transcendentals=0),
    )(rows, shift_row, scale_row)


def head_norm(values, gain):
    return (values * lax.rsqrt(jnp.mean(values * values, -1, keepdims=True) + 1e-06) * gain).astype(
        jnp.bfloat16
    )


def stale_kernel(n_rows, patch, plan_ref, *refs):
    row_refs = refs[:n_rows]
    w_ref, kv_ref, q_gain_ref, k_gain_ref, q_out, fresh_out, top_out, den_out, num_out = refs[n_rows:]
    head = kv_ref.shape[2] // 2
    scale = score_scale(head)
    rows = [r[...] for r in row_refs]
    rows = jnp.concatenate(rows, 0) if n_rows > 1 else rows[0]
    qkv = jnp.dot(rows, w_ref[0], preferred_element_type=jnp.float32)
    query = head_norm(qkv[:, :head], q_gain_ref[...])
    q_out[0] = query
    fresh_out[0, :, :head] = head_norm(qkv[:, head : 2 * head], k_gain_ref[...])
    fresh_out[0, :, head:] = qkv[:, 2 * head :].astype(jnp.bfloat16)
    plan = plan_ref[0]
    ones = jnp.ones((patch, head), jnp.bfloat16)
    top = None
    for j in range(kv_ref.shape[1] // patch - 1):
        block = j + (j >= plan).astype(jnp.int32)
        at = pl.ds(pl.multiple_of(block * patch, patch), patch)
        scores = lax.dot_general(query, kv_ref[0, at, :head], NT, preferred_element_type=jnp.float32)
        new_top = jnp.max(scores, -1, keepdims=True) * scale
        if top is not None:
            new_top = jnp.maximum(top, new_top)
        weights = jnp.exp2(scores * scale - new_top).astype(jnp.bfloat16)
        values = jnp.concatenate([kv_ref[0, at, head:], ones], 1)
        term = jnp.dot(weights, values, preferred_element_type=jnp.float32)
        total = term if top is None else total * jnp.exp2(top - new_top) + term
        top = new_top
    top_out[0] = jnp.broadcast_to(top, top_out.shape[1:])
    num_out[0] = total[:, :head]
    den_out[0] = total[:, head:]


def stale_part(plan, rows, weight, kv, q_gain, k_gain):
    heads, width, cols = weight.shape
    seq, pair = kv.shape[1:]
    head = pair // 2
    count = sum(r.shape[0] for r in rows)
    patch = 512

    def whole(a):
        return pl.BlockSpec(a.shape, lambda h, p: (0,) * a.ndim)

    def by_head(*shape):
        return pl.BlockSpec((1,) + shape, lambda h, p: (h, 0, 0))

    flat = jax.ShapeDtypeStruct((heads, count, head), jnp.float32)
    return pl.pallas_call(
        functools.partial(stale_kernel, len(rows), patch),
        grid_spec=pltpu.PrefetchScalarGridSpec(
            num_scalar_prefetch=1,
            grid=(heads,),
            in_specs=[whole(r) for r in rows]
            + [by_head(width, cols), by_head(seq, pair), whole(q_gain), whole(k_gain)],
            out_specs=[by_head(count, head), by_head(count, pair)] + [by_head(count, head)] * 3,
        ),
        out_shape=[
            jax.ShapeDtypeStruct((heads, count, head), jnp.bfloat16),
            jax.ShapeDtypeStruct((heads, count, pair), jnp.bfloat16),
            flat,
            flat,
            flat,
        ],
        compiler_params=pltpu.CompilerParams(vmem_limit_bytes=40 * MIB),
        cost_estimate=pl.CostEstimate(
            flops=2 * count * heads * (width * cols + seq * pair),
            bytes_accessed=13 * MIB,
            transcendentals=count * heads * seq,
        ),
    )(plan, *rows, weight, kv, q_gain, k_gain)


def fresh_kernel(q_ref, top_ref, den_ref, num_ref, fresh_ref, w_ref, term_ref):
    heads, count = q_ref.shape[0], fresh_ref.shape[1]
    head = q_ref.shape[2]
    scale = score_scale(head)
    ones = jnp.ones((count, head), jnp.bfloat16)
    parts = []
    for h in range(heads):
        scores = lax.dot_general(q_ref[h], fresh_ref[h, :, :head], NT, preferred_element_type=jnp.float32)
        top = top_ref[h]
        new_top = jnp.maximum(top, jnp.max(scores, -1, keepdims=True) * scale)
        weights = jnp.exp2(scores * scale - jnp.concatenate([new_top] * (count // head), 1))
        values = jnp.concatenate([fresh_ref[h, :, head:], ones], 1)
        term = jnp.dot(weights.astype(jnp.bfloat16), values, preferred_element_type=jnp.float32)
        shrink = jnp.exp2(top - new_top)
        num = num_ref[h] * shrink + term[:, :head]
        den = den_ref[h] * shrink + term[:, head:]
        parts.append((num / den).astype(jnp.bfloat16))
    attn = jnp.concatenate(parts, 1)
    term_ref[...] = jnp.dot(attn, w_ref[...], preferred_element_type=jnp.float32).astype(jnp.bfloat16)


def fresh_part(query, top, den, num, fresh, weight):
    heads, count, head = query.shape
    return pl.pallas_call(
        fresh_kernel,
        out_shape=jax.ShapeDtypeStruct((count, weight.shape[1]), jnp.bfloat16),
        compiler_params=pltpu.CompilerParams(vmem_limit_bytes=40 * MIB),
        cost_estimate=pl.CostEstimate(
            flops=2 * count * (weight.size + 2 * heads * fresh.shape[1] * head),
            bytes_accessed=4 * MIB,
            transcendentals=count * heads * fresh.shape[1],
        ),
    )(query, top, den, num, fresh, weight)


def on_device(
    incoming, plan, stale_kv, qkv_weight, out_weight, q_gain, k_gain, shift_mod, scale_mod, gate_mod
):
    kv = jnp.transpose(stale_kv[0], (1, 0, 2))
    weight = jnp.transpose(qkv_weight[0], (1, 0, 2))
    w_rows = out_weight[0].reshape(-1, out_weight.shape[3])
    blocks = lax.axis_size("section")
    own = lax.ppermute(incoming[0], "section", [((i - 1) % blocks, i) for i in range(blocks)])
    modulated = normalize(own, shift_mod, scale_mod)
    rows = lax.all_gather(modulated, "ulysses", axis=0, tiled=True)
    query, fresh, top, den, num = stale_part(plan, [rows], weight, kv, q_gain, k_gain)
    term = fresh_part(query, top, den, num, fresh, w_rows)
    proj = lax.psum_scatter(term, "ulysses", scatter_dimension=0, tiled=True).astype(jnp.float32)
    block_out = own + gate_mod[0] * proj
    return (block_out[None], jnp.transpose(fresh, (1, 0, 2))[None])


def solution(mesh):
    return jax.shard_map(
        on_device,
        mesh=mesh,
        in_specs=(
            P(("batch", "section"), "ulysses", None),
            P("section"),
            P(("batch", "section"), None, "ulysses", None),
            P("section", None, "ulysses", None),
            P("section", "ulysses", None, None),
            P("section", None),
            P("section", None),
            P("section", None),
            P("section", None),
            P("section", None),
        ),
        out_specs=(
            P(("batch", "section"), "ulysses", None),
            P(("batch", "section"), None, "ulysses", None),
        ),
        check_vma=False,
    )
```

```python
import functools
import math

import jax
import jax.numpy as jnp
from jax import lax
from jax.experimental import pallas as pl
from jax.experimental.pallas import tpu as pltpu
from jax.sharding import PartitionSpec as P

NT = (((1,), (1,)), ((), ()))
MIB = 2**20


def score_scale(head_size):
    return math.log2(math.e) / math.sqrt(head_size)


def norm_kernel(x_ref, shift_ref, scale_ref, first_ref, second_ref):
    rows = x_ref[...]
    centered = rows - jnp.mean(rows, -1, keepdims=True)
    var = jnp.mean(centered * centered, -1, keepdims=True)
    modulated = (
        centered * lax.rsqrt(var + 1e-06) * (1.0 + scale_ref[...]) + shift_ref[...]
    ).astype(jnp.bfloat16)
    half = first_ref.shape[0]
    first_ref[...] = modulated[:half]
    second_ref[...] = modulated[half:]


def normalize(rows, shift_row, scale_row):
    return pl.pallas_call(
        norm_kernel,
        out_shape=[jax.ShapeDtypeStruct((rows.shape[0] // 2, rows.shape[1]), jnp.bfloat16)] * 2,
        cost_estimate=pl.CostEstimate(flops=8 * rows.size, bytes_accessed=6 * rows.size, transcendentals=0),
    )(rows, shift_row, scale_row)


def head_norm(values, gain):
    return (values * lax.rsqrt(jnp.mean(values * values, -1, keepdims=True) + 1e-06) * gain).astype(
        jnp.bfloat16
    )


def project_rows(row_refs, w_ref, q_gain_ref, k_gain_ref, q_out, fresh_out):
    head = q_out.shape[2]
    rows = [r[...] for r in row_refs]
    rows = jnp.concatenate(rows, 0) if len(rows) > 1 else rows[0]
    qkv = jnp.dot(rows, w_ref[0], preferred_element_type=jnp.float32)
    query = head_norm(qkv[:, :head], q_gain_ref[...])
    q_out[0] = query
    fresh_out[0, :, :head] = head_norm(qkv[:, head : 2 * head], k_gain_ref[...])
    fresh_out[0, :, head:] = qkv[:, 2 * head :].astype(jnp.bfloat16)
    return query


def attend_stale(patch, plan, query, kv_ref, top_out, den_out, num_out):
    head = query.shape[1]
    scale = score_scale(head)
    ones = jnp.ones((patch, head), jnp.bfloat16)
    top = None
    for j in range(kv_ref.shape[1] // patch - 1):
        block = j + (j >= plan).astype(jnp.int32)
        at = pl.ds(pl.multiple_of(block * patch, patch), patch)
        scores = lax.dot_general(query, kv_ref[0, at, :head], NT, preferred_element_type=jnp.float32)
        new_top = jnp.max(scores, -1, keepdims=True) * scale
        if top is not None:
            new_top = jnp.maximum(top, new_top)
        weights = jnp.exp2(scores * scale - new_top).astype(jnp.bfloat16)
        values = jnp.concatenate([kv_ref[0, at, head:], ones], 1)
        term = jnp.dot(weights, values, preferred_element_type=jnp.float32)
        total = term if top is None else total * jnp.exp2(top - new_top) + term
        top = new_top
    top_out[0] = jnp.broadcast_to(top, top_out.shape[1:])
    num_out[0] = total[:, :head]
    den_out[0] = total[:, head:]


def whole(a):
    return pl.BlockSpec(a.shape, lambda h, *p: (0,) * a.ndim)


def by_head(*shape):
    return pl.BlockSpec((1,) + shape, lambda h, *p: (h, 0, 0))


def both_kernel(n_rows, patch, plan_ref, *refs):
    w_ref, kv_ref, q_gain_ref, k_gain_ref, q_out, fresh_out, top_out, den_out, num_out = refs[n_rows:]
    query = project_rows(refs[:n_rows], w_ref, q_gain_ref, k_gain_ref, q_out, fresh_out)
    attend_stale(patch, plan_ref[0], query, kv_ref, top_out, den_out, num_out)


def project_and_attend(patch, plan, rows, weight, kv, q_gain, k_gain):
    heads, width, cols = weight.shape
    seq, pair = kv.shape[1:]
    head = pair // 2
    count = sum(r.shape[0] for r in rows)
    flat = jax.ShapeDtypeStruct((heads, count, head), jnp.float32)
    return pl.pallas_call(
        functools.partial(both_kernel, len(rows), patch),
        grid_spec=pltpu.PrefetchScalarGridSpec(
            num_scalar_prefetch=1,
            grid=(heads,),
            in_specs=[whole(r) for r in rows]
            + [by_head(width, cols), by_head(seq, pair), whole(q_gain), whole(k_gain)],
            out_specs=[by_head(count, head), by_head(count, pair)] + [by_head(count, head)] * 3,
        ),
        out_shape=[
            jax.ShapeDtypeStruct((heads, count, head), jnp.bfloat16),
            jax.ShapeDtypeStruct((heads, count, pair), jnp.bfloat16),
            flat,
            flat,
            flat,
        ],
        compiler_params=pltpu.CompilerParams(vmem_limit_bytes=24 * MIB),
        cost_estimate=pl.CostEstimate(
            flops=2 * count * heads * (width * cols + seq * pair),
            bytes_accessed=13 * MIB,
            transcendentals=count * heads * seq,
        ),
    )(plan, *rows, weight, kv, q_gain, k_gain)


def project_kernel(n_rows, *refs):
    w_ref, q_gain_ref, k_gain_ref, q_out, fresh_out = refs[n_rows:]
    project_rows(refs[:n_rows], w_ref, q_gain_ref, k_gain_ref, q_out, fresh_out)


def project(rows, weight, q_gain, k_gain):
    heads, width, cols = weight.shape
    head = cols // 3
    count = sum(r.shape[0] for r in rows)
    return pl.pallas_call(
        functools.partial(project_kernel, len(rows)),
        grid=(heads,),
        in_specs=[whole(r) for r in rows] + [by_head(width, cols), whole(q_gain), whole(k_gain)],
        out_specs=[by_head(count, head), by_head(count, 2 * head)],
        out_shape=[
            jax.ShapeDtypeStruct((heads, count, head), jnp.bfloat16),
            jax.ShapeDtypeStruct((heads, count, 2 * head), jnp.bfloat16),
        ],
        compiler_params=pltpu.CompilerParams(vmem_limit_bytes=16 * MIB),
        cost_estimate=pl.CostEstimate(
            flops=2 * count * weight.size, bytes_accessed=7 * MIB, transcendentals=0
        ),
    )(*rows, weight, q_gain, k_gain)


def stale_kernel(patch, plan_ref, q_ref, kv_ref, top_out, den_out, num_out):
    attend_stale(patch, plan_ref[0], q_ref[0], kv_ref, top_out, den_out, num_out)


def attend(patch, plan, query, kv):
    heads, count, head = query.shape
    seq = kv.shape[1]
    return pl.pallas_call(
        functools.partial(stale_kernel, patch),
        grid_spec=pltpu.PrefetchScalarGridSpec(
            num_scalar_prefetch=1,
            grid=(heads,),
            in_specs=[by_head(count, head), by_head(seq, 2 * head)],
            out_specs=[by_head(count, head)] * 3,
        ),
        out_shape=[jax.ShapeDtypeStruct((heads, count, head), jnp.float32)] * 3,
        compiler_params=pltpu.CompilerParams(vmem_limit_bytes=16 * MIB),
        cost_estimate=pl.CostEstimate(
            flops=4 * query.size * seq, bytes_accessed=6 * MIB, transcendentals=count * heads * seq
        ),
    )(plan, query, kv)


def fresh_kernel(n_fresh, q_ref, top_ref, den_ref, num_ref, w_ref, *refs):
    fresh_refs, term_refs = refs[:n_fresh], refs[n_fresh:]
    heads, _, head = q_ref.shape
    count = sum(r.shape[1] for r in fresh_refs)
    scale = score_scale(head)
    ones = jnp.ones((count, head), jnp.bfloat16)
    parts = []
    for h in range(heads):
        fresh = jnp.concatenate([r[h] for r in fresh_refs], 0)
        scores = lax.dot_general(q_ref[h], fresh[:, :head], NT, preferred_element_type=jnp.float32)
        top = top_ref[h]
        new_top = jnp.maximum(top, jnp.max(scores, -1, keepdims=True) * scale)
        weights = jnp.exp2(scores * scale - jnp.concatenate([new_top] * (count // head), 1))
        values = jnp.concatenate([fresh[:, head:], ones], 1)
        term = jnp.dot(weights.astype(jnp.bfloat16), values, preferred_element_type=jnp.float32)
        shrink = jnp.exp2(top - new_top)
        num = num_ref[h] * shrink + term[:, :head]
        den = den_ref[h] * shrink + term[:, head:]
        parts.append((num / den).astype(jnp.bfloat16))
    attn = jnp.concatenate(parts, 1)
    terms = jnp.dot(attn, w_ref[...], preferred_element_type=jnp.float32).astype(jnp.bfloat16)
    size = term_refs[0].shape[0]
    for i, r in enumerate(term_refs):
        r[...] = terms[i * size : (i + 1) * size]


def fresh_terms(state, fresh, weight, pieces):
    query = state[0]
    heads, count, head = query.shape
    total = sum(f.shape[1] for f in fresh)
    return pl.pallas_call(
        functools.partial(fresh_kernel, len(fresh)),
        out_shape=[jax.ShapeDtypeStruct((count // pieces, weight.shape[1]), jnp.bfloat16)] * pieces,
        compiler_params=pltpu.CompilerParams(vmem_limit_bytes=16 * MIB),
        cost_estimate=pl.CostEstimate(
            flops=2 * count * (weight.size + 2 * heads * total * head),
            bytes_accessed=4 * MIB,
            transcendentals=count * heads * total,
        ),
    )(*state, weight, *fresh)


def join(partial, term):
    return (partial.astype(jnp.float32) + term.astype(jnp.float32)).astype(jnp.bfloat16)


def on_device(
    incoming, plan, stale_kv, qkv_weight, out_weight, q_gain, k_gain, shift_mod, scale_mod, gate_mod
):
    kv = jnp.transpose(stale_kv[0], (1, 0, 2))
    weight = jnp.transpose(qkv_weight[0], (1, 0, 2))
    w_rows = out_weight[0].reshape(-1, out_weight.shape[3])
    blocks, ring = lax.axis_size("section"), lax.axis_size("ulysses")
    rank = lax.axis_index("ulysses")
    shard = incoming.shape[1]
    half, patch = shard // 2, shard * ring
    far = ring // 2

    def up(chunk):
        return lax.ppermute(chunk, "ulysses", [(i, (i + 1) % ring) for i in range(ring)])

    def down(chunk):
        return lax.ppermute(chunk, "ulysses", [((i + 1) % ring, i) for i in range(ring)])

    own = lax.ppermute(incoming[0], "section", [((i - 1) % blocks, i) for i in range(blocks)])
    first, second = normalize(own, shift_mod, scale_mod)

    below, above = {0: (first, second)}, {0: (first, second)}
    for d in range(1, far):
        below[d] = (up(below[d - 1][0]), up(below[d - 1][1]))
        b = down(above[d - 1][1])
        above[d] = (down(above[d - 1][0]), b)
    last = (up(below[far - 1][0]), down(above[far - 1][1]))

    groups = [project_and_attend(patch, plan, [first, second], weight, kv, q_gain, k_gain)]
    for d in range(1, far):
        groups.append(
            project_and_attend(patch, plan, [*below[d], *above[d]], weight, kv, q_gain, k_gain)
        )
    last_query, last_fresh = project(last, weight, q_gain, k_gain)
    fresh = [g[1] for g in groups] + [last_fresh]

    def terms(state, pieces):
        return fresh_terms((state[0], *state[2:]), fresh, w_rows, pieces)

    low_a, low_b, high_a, high_b = terms(groups[far - 1], 4)
    up_b, down_a = up(high_b), down(low_a)
    last_state = (last_query, last_fresh, *attend(patch, plan, last_query, kv))
    far_a, far_b = terms(last_state, 2)
    up_a, down_b = up(far_a), down(far_b)
    for d in range(far - 1, 0, -1):
        up_a, down_b = up(join(up_a, high_a)), down(join(down_b, low_b))
        if d > 1:
            low_a, low_b, high_a, high_b = terms(groups[d - 1], 4)
            up_b, down_a = up(join(up_b, high_b)), down(join(down_a, low_a))
    own_a, own_b = terms(groups[0], 2)

    def total(a, b, c):
        return a.astype(jnp.float32) + b.astype(jnp.float32) + c.astype(jnp.float32)

    proj = jnp.concatenate([total(own_a, up_a, down_a), total(own_b, up_b, down_b)], 0)
    block_out = own + gate_mod[0] * proj

    shards = [f[:, :shard] for f in fresh[far - 1 : 0 : -1]] + [fresh[0]]
    shards += [f[:, shard:] for f in fresh[1:far]] + [last_fresh]
    twice = jnp.concatenate(shards + shards, 1)
    start = (far - 1 - rank) % ring * shard
    ordered = lax.dynamic_slice_in_dim(twice, start, patch, 1)
    return (block_out[None], jnp.transpose(ordered, (1, 0, 2))[None])


def solution(mesh):
    return jax.shard_map(
        on_device,
        mesh=mesh,
        in_specs=(
            P(("batch", "section"), "ulysses", None),
            P("section"),
            P(("batch", "section"), None, "ulysses", None),
            P("section", None, "ulysses", None),
            P("section", "ulysses", None, None),
            P("section", None),
            P("section", None),
            P("section", None),
            P("section", None),
            P("section", None),
        ),
        out_specs=(
            P(("batch", "section"), "ulysses", None),
            P(("batch", "section"), None, "ulysses", None),
        ),
        check_vma=False,
    )
```
